256 devices in a mesh: ctx: 32 (over x, y, core), tp: 8 (over z).
Axes of the slice: x: 4, y: 4, z: 8, core: 2. Of those that a mesh axis runs over, the one named last changes fastest.
Arguments:
- routed_x: bfloat16 [12288, 4096], P('ctx', 'tp'), may hold values from -20 to 20
- norm_gain: float32 [4096], replicated, may hold values from 0.1 to 1.9
- w_query: bfloat16 [4096, 4096], P(None, 'tp'), may hold values from -16 to 16
- w_key: bfloat16 [4096, 1024], P(None, 'tp'), may hold values from -1 to 1
- w_value: bfloat16 [4096, 1024], P(None, 'tp'), may hold values from -0.09375 to 0.09375
- w_out: bfloat16 [4096, 4096], P('tp'), may hold values from -0.5 to 0.5
- positions: int32 [12288], P('ctx'), may hold values from 0 to 262143, as said below
- counts: int32 [32], P('ctx'), may hold values from 96 to 384, as said below
- router_weight: float32 [12288], P('ctx'), may hold values from 0.25 to 1
Outputs:
- update: bfloat16 [12288, 4096], P('ctx', 'tp')
The draws below stay inside these ranges and needn't reach their ends.
Inputs may be any that keep to these rules, and one draw needn't show every extreme that they name: Shard s's first counts[s] slots hold distinct increasing positions in [s * 8192, (s + 1) * 8192); its other slots hold 0. `counts`: each between 96 and 384; some shard has exactly 384.
All inputs are finite; a program needn't handle non-finite values.
Results may differ from the reference program's by a relative error of at most 0.02.
Values may be sent and summed in bfloat16 or wider, within the bound.
A program may use at most 128 MiB of HBM per device.

```python
import math
import jax
import jax.numpy as jnp
from jax import lax

D = 4096
HEADS = 32
KV_HEADS = 8
HD = 128
TOK_DEV = 8192
CAP = 384
ROWS = 12288
TOKENS = 262144
N_CTX = 32
N_TP = 8


def routing_plan(key):
    count_key = jax.random.fold_in(key, 101)
    drawn = jax.random.randint(count_key, (N_CTX,), CAP // 4, CAP + 1)
    chosen = jax.random.randint(jax.random.fold_in(key, 102), (), 0, N_CTX)
    shard_ids = jnp.arange(N_CTX, dtype=jnp.int32)
    counts = jnp.where(shard_ids == chosen, CAP, drawn).astype(jnp.int32)
    shard_keys = jax.random.split(jax.random.fold_in(key, 103), N_CTX)
    offsets = jax.vmap(lambda one_key: jax.random.permutation(one_key, TOK_DEV)[:CAP])(shard_keys)
    slot_index = jnp.arange(CAP, dtype=jnp.int32)
    is_live = slot_index[None, :] < counts[:, None]
    offsets = jnp.sort(jnp.where(is_live, offsets, TOK_DEV), axis=1)
    placed = jnp.where(is_live, offsets + shard_ids[:, None] * TOK_DEV, 0)
    return (counts, placed.reshape(-1).astype(jnp.int32))


def key_base(key):
    return jnp.clip(jax.random.normal(jax.random.fold_in(key, 201), (D, KV_HEADS * HD), jnp.float32), -6.0, 6.0)


def draw_counts(key, part):
    counts, placed = routing_plan(key)
    return counts


def draw_positions(key, part):
    counts, placed = routing_plan(key)
    return placed


def draw_w_key(key, part):
    base = key_base(key)
    return (base / math.sqrt(D)).astype(jnp.bfloat16)


def draw_w_query(key, part):
    key = jax.random.fold_in(key, 5)
    noise = jnp.clip(jax.random.normal(key, (D, HEADS * HD), jnp.float32), -6.0, 6.0)
    return (noise / math.sqrt(D)).astype(jnp.bfloat16)


def draw_routed_x(key, part):
    key = jax.random.fold_in(key, 9)
    return jnp.clip(jax.random.normal(key, (CAP * N_CTX, D), jnp.float32), -6.0, 6.0).astype(jnp.bfloat16)


def levels(rng, extent, shards, low, top_value):
    gain = 1.0
    for position, blocks in shards:
        draws = jax.random.uniform(jax.random.fold_in(jax.random.fold_in(rng, 6), position), (blocks,), jnp.float32, low / len(shards), top_value / len(shards))
        gain = gain * jnp.repeat(jnp.exp(draws), extent[position] // blocks).reshape((-1,) + (1,) * (len(extent) - 1 - position))
    return gain


def bell_draw(stream_key, shape, deviation, reach, shards=(), held_as=jnp.bfloat16):
    factor_of = levels(stream_key, shape, shards, -0.22, 0.18) if shards else 1.0
    array = jax.random.normal(stream_key, shape, jnp.float32) * deviation * factor_of
    return jnp.minimum(jnp.maximum(array, -reach), reach).astype(held_as)


def setup_inputs(seed: int = 0) -> dict:
    key_of = jax.random.split(jax.random.key(seed), 10)
    routed_x = draw_routed_x(jax.random.fold_in(key_of[9], 71), 0)
    norm_gain = jnp.clip(1.0 + 0.18 * jax.random.normal(key_of[1], (D,), jnp.float32), 0.1, 1.9)
    w_query = draw_w_query(jax.random.fold_in(key_of[9], 71), 0)
    w_key = draw_w_key(jax.random.fold_in(key_of[9], 71), 0)
    w_value = bell_draw(key_of[4], (D, KV_HEADS * HD), D ** -0.5, 0.09375, ((1, 8),))
    w_out = bell_draw(key_of[5], (HEADS * HD, D), HD ** -0.5, 0.5, ((0, 8),))
    positions = draw_positions(jax.random.fold_in(key_of[9], 71), 0)
    counts = draw_counts(jax.random.fold_in(key_of[9], 71), 0)
    router_weight = jnp.clip(0.25 + 0.75 * jax.random.uniform(key_of[8], (ROWS,), jnp.float32) ** levels(key_of[8], (ROWS,), ((0, 32),), -0.2, 0.2), 0.25, 1.0)
    return {"routed_x": routed_x, "norm_gain": norm_gain, "w_query": w_query, "w_key": w_key, "w_value": w_value, "w_out": w_out, "positions": positions, "counts": counts, "router_weight": router_weight}


def reference(routed_x, norm_gain, w_query, w_key, w_value, w_out, positions, counts, router_weight):
    row_count = routed_x.shape[0]
    widened = routed_x.astype(jnp.float32)
    normed = (widened * lax.rsqrt(lax.optimization_barrier(jnp.mean(widened * widened, axis=-1, keepdims=True)) + 1e-05) * norm_gain).astype(jnp.bfloat16)
    queries = jnp.dot(normed, w_query, preferred_element_type=jnp.float32).astype(jnp.bfloat16)
    key_rows = jnp.dot(normed, w_key, preferred_element_type=jnp.float32).astype(jnp.bfloat16)
    value_rows = jnp.dot(normed, w_value, preferred_element_type=jnp.float32).astype(jnp.bfloat16)
    slot_index = jnp.arange(row_count, dtype=jnp.int32)
    shard_index = slot_index // CAP
    is_live = slot_index % CAP < counts[shard_index]
    query_pos = jnp.where(is_live, positions, TOKENS).astype(jnp.int32)
    key_pos = jnp.where(is_live, positions, TOKENS + 1).astype(jnp.int32)
    group_size = HEADS // KV_HEADS
    key_heads = key_rows.astype(jnp.float32).reshape(row_count, KV_HEADS, HD).transpose(1, 0, 2)
    value_heads = value_rows.astype(jnp.float32).reshape(row_count, KV_HEADS, HD).transpose(1, 0, 2)
    query_blocks = queries.astype(jnp.float32).reshape(N_CTX, CAP, KV_HEADS, group_size, HD).transpose(0, 2, 1, 3, 4)
    qpos_blocks = query_pos.reshape(N_CTX, CAP)
    scale = HD ** (-0.5)

    def one_block(block_item):
        query_block, qpos_block = block_item
        allowed = key_pos[None, :] <= qpos_block[:, None]

        def one_head(head_item):
            query_head, key_head, value_head = head_item
            scores = jnp.einsum('qgd,nd->gqn', query_head, key_head) * scale
            masked = jnp.where(allowed[None], scores, -1e+30)
            row_max = lax.optimization_barrier(jnp.max(masked, axis=-1, keepdims=True))
            weights = jnp.where(allowed[None], jnp.exp(masked - row_max), 0.0)
            totals = lax.optimization_barrier(jnp.sum(weights, axis=-1, keepdims=True))
            rounded = lax.optimization_barrier(weights.astype(jnp.bfloat16)).astype(jnp.float32)
            mixed = jnp.einsum('gqn,nd->gqd', rounded, value_head) / totals
            return mixed.astype(jnp.bfloat16)
        per_head = lax.map(one_head, (query_block, key_heads, value_heads))
        return per_head.transpose(2, 0, 1, 3).reshape(CAP, HEADS * HD)
    heads_out = lax.map(one_block, (query_blocks, qpos_blocks)).reshape(row_count, HEADS * HD)
    head_width = HEADS * HD // N_TP
    summed = jnp.zeros((row_count, D), jnp.float32)
    for member in range(N_TP):
        partial_term = jnp.dot(heads_out[:, member * head_width:(member + 1) * head_width], w_out[member * head_width:(member + 1) * head_width], preferred_element_type=jnp.float32).astype(jnp.bfloat16)
        summed = summed + lax.optimization_barrier(partial_term).astype(jnp.float32)
    update = jnp.where(is_live[:, None], router_weight[:, None] * summed, 0.0)
    return update.astype(jnp.bfloat16)
```

```python
import jax
import jax.numpy as jnp
from jax import lax
from jax.experimental import pallas as pl
from jax.experimental.pallas import tpu as pltpu
from jax.sharding import PartitionSpec as P

HD = 128
GROUP = 4
ROWS = 384
CHUNK = 128
CHUNKS = 3
FEATURES = 512
Q_ROWS = GROUP * CHUNK
K_TILE = HD + 16
NX, NY, NZ = 4, 4, 8
NEG = -1e30
LOG2E = 1.4426950408889634
BF16 = jnp.bfloat16
F32 = jnp.float32

SCHEDULE = (
    ["zs00", "zs10", "own", "z01", "zs20", "z02", "z11", "z03", "z12", "z04", "fin0", "kva0"]
    + ["z13", "kvb0", "z21", "kvc0", "z14", "fin1", "kva1", "kvd0", "z22", "kvb1", "kve0"]
    + ["z23", "kvc1", "kvf0", "kvd1", "at00", "z24", "fin2", "kva2", "kve1", "kvf1"]
    + ["at01", "kvb2", "at10", "kvc2", "at11", "kvd2", "at20", "kve2", "at21", "kvf2"]
    + ["at02", "ho0", "rs01", "at12", "ho1", "rs02", "rs11", "at22", "ho2", "rs03", "rs12", "rs21"]
    + ["rs04", "rs13", "rs22", "rs05", "rs14", "rs23", "rs15", "rs24", "rs25"]
)


def dot(a, b):
    return jnp.dot(a, b, preferred_element_type=F32)


def kernel(
    x_ref, gain_ref, wq_hbm, wk_hbm, wv_hbm, wo_hbm, count_ref, router_ref, out_ref,
    xg, wq, wkv, wo, acc_q, acc_kv, ssq, qs, kt, va, m_s, l_s, o_s, ho, sb, rb,
    w_sem, z_send, z_recv, kv_send, kv_recv, sib_send, sib_recv, rs_send, rs_recv,
):
    ctx = lax.axis_index("ctx")
    t = lax.axis_index("tp")
    core = lax.rem(ctx, 2)
    y = lax.rem(lax.div(ctx, 2), NY)
    x = lax.div(ctx, 2 * NY)

    def at(xx, yy, cc, tt):
        return ((lax.rem(xx, NX) * NY + lax.rem(yy, NY)) * 2 + cc, lax.rem(tt, NZ))

    z_next = (at(x, y, core, t + 1), at(x, y, core, t + NZ - 1))
    x_next = (at(x + 1, y, core, t), at(x + NX - 1, y, core, t))
    y_next = (at(x, y + 1, core, t), at(x, y + NY - 1, core, t))
    sibling = at(x, y, 1 - core, t)
    count = count_ref[0]

    weights = [
        pltpu.make_async_copy(wq_hbm, wq, w_sem.at[0]),
        pltpu.make_async_copy(wk_hbm, wkv.at[:, pl.ds(0, HD)], w_sem.at[1]),
        pltpu.make_async_copy(wv_hbm, wkv.at[:, pl.ds(HD, HD)], w_sem.at[2]),
        pltpu.make_async_copy(wo_hbm, wo, w_sem.at[3]),
    ]
    for copy in weights:
        copy.start()

    barrier = pltpu.get_barrier_semaphore()
    peers = z_next + x_next + y_next + (sibling,)
    for peer in peers:
        pl.semaphore_signal(barrier, inc=1, device_id=peer, device_id_type=pl.DeviceIdType.MESH)
    pl.semaphore_wait(barrier, len(peers))

    sends = []

    def remote(src, dst, send_sem, recv_sem, device):
        return pltpu.make_async_remote_copy(
            src_ref=src, dst_ref=dst, send_sem=send_sem, recv_sem=recv_sem,
            device_id=device, device_id_type=pl.DeviceIdType.MESH,
        )

    def send(src, dst, send_sem, recv_sem, device):
        copy = remote(src, dst, send_sem, recv_sem, device)
        copy.start()
        sends.append(copy)

    def arrived(dst, send_sem, recv_sem, device):
        remote(dst, dst, send_sem, recv_sem, device).wait_recv()

    def z_rows(d, k, h):
        if h < 4:
            return pl.ds(k * CHUNK, CHUNK)
        return pl.ds(k * CHUNK + d * (CHUNK // 2), CHUNK // 2)

    def z_start(k, h):
        for d, sign in enumerate((1, -1)):
            block = lax.rem(t - sign * (h - 1) + NZ, NZ)
            dst = xg.at[block, z_rows(d, k, h)]
            src = x_ref.at[z_rows(d, k, h)] if h == 1 else dst
            send(src, dst, z_send.at[d, k, h - 1], z_recv.at[d, k, h - 1], z_next[d])

    def project(block, values, rows):
        widened = values.astype(F32)
        squares = widened * widened
        ssq[rows] += sum(squares[:, i * 128 : (i + 1) * 128] for i in range(FEATURES // 128))
        scaled = (widened * gain_ref[block]).astype(BF16)
        features = pl.ds(pl.multiple_of(block * FEATURES, FEATURES), FEATURES)
        acc_q[rows] += dot(scaled, wq[features])
        acc_kv[rows] += dot(scaled, wkv[features])

    def z_step(k, h):
        for d, sign in enumerate((1, -1)):
            block = lax.rem(t - sign * h + NZ, NZ)
            arrived(
                xg.at[block, z_rows(d, k, h)], z_send.at[d, k, h - 1], z_recv.at[d, k, h - 1], z_next[d]
            )
        if h < 4:
            z_start(k, h + 1)
        rows = pl.ds(k * CHUNK, CHUNK)
        for sign in (1, -1) if h < 4 else (1,):
            block = lax.rem(t - sign * h + NZ, NZ)
            project(block, xg[block, rows], rows)

    def own():
        for copy in weights[:3]:
            copy.wait()
        ssq[...] = jnp.zeros_like(ssq)
        acc_q[...] = jnp.zeros_like(acc_q)
        acc_kv[...] = jnp.zeros_like(acc_kv)
        m_s[...] = jnp.full_like(m_s, NEG)
        l_s[...] = jnp.zeros_like(l_s)
        o_s[...] = jnp.zeros_like(o_s)
        project(t, x_ref[...], pl.ds(0, ROWS))

    def finish(k):
        rows = pl.ds(k * CHUNK, CHUNK)
        mean = jnp.sum(ssq[rows], axis=1, keepdims=True) * (1.0 / (NZ * FEATURES))
        inverse = lax.rsqrt(mean + 1e-05)
        query = (acc_q[rows] * (inverse * (HD**-0.5 * LOG2E))).astype(BF16)
        for h in range(GROUP):
            qs[k, h * CHUNK : (h + 1) * CHUNK, :] = query[:, h * HD : (h + 1) * HD]
        pair = acc_kv[rows] * inverse
        kt[k, core, y, x, 0:HD, :] = jnp.transpose(pair[:, :HD]).astype(BF16)
        slot = lax.broadcasted_iota(jnp.int32, (16, CHUNK), 1) + k * CHUNK
        kt[k, core, y, x, HD:K_TILE, :] = jnp.where(slot < count, 0.0, NEG).astype(BF16)
        va[k, core, x, y, :, :] = pair[:, HD:].astype(BF16)

    kinds = (
        (kt, x, y, x_next, y_next, ((0, 80), (80, 64))),
        (va, y, x, y_next, x_next, ((0, 64), (64, 64))),
    )

    def kv_sems(k, a, phase, d, hop):
        return kv_send.at[k, a, phase, d, hop], kv_recv.at[k, a, phase, d, hop]

    def kva(k):
        for a, (buf, inner, outer, inner_next, outer_next, parts) in enumerate(kinds):
            tile = buf.at[k, core, outer, inner]
            for d in range(2):
                send(tile, tile, *kv_sems(k, a, 0, d, 0), inner_next[d])

    def kvb(k):
        for a, (buf, inner, outer, inner_next, outer_next, parts) in enumerate(kinds):
            for d in range(2):
                source = lax.rem(inner + (3, 1)[d], 4)
                tile = buf.at[k, core, outer, source]
                arrived(tile, *kv_sems(k, a, 0, d, 0), inner_next[d])
                part = buf.at[k, core, outer, source, pl.ds(*parts[d])]
                send(part, part, *kv_sems(k, a, 0, d, 1), inner_next[d])

    def kvc(k):
        for a, (buf, inner, outer, inner_next, outer_next, parts) in enumerate(kinds):
            for d in range(2):
                source = lax.rem(inner + 2, 4)
                part = buf.at[k, core, outer, source, pl.ds(*parts[d])]
                arrived(part, *kv_sems(k, a, 0, d, 1), inner_next[d])
            line = buf.at[k, core, outer]
            for d in range(2):
                send(line, line, *kv_sems(k, a, 1, d, 0), outer_next[d])
            send(line, line, sib_send.at[k, a, 0], sib_recv.at[k, a, 0], sibling)

    def kvd(k):
        for a, (buf, inner, outer, inner_next, outer_next, parts) in enumerate(kinds):
            for d in range(2):
                source = lax.rem(outer + (3, 1)[d], 4)
                line = buf.at[k, core, source]
                arrived(line, *kv_sems(k, a, 1, d, 0), outer_next[d])
                part = buf.at[k, core, source, pl.ds(2 * d, 2)]
                send(part, part, *kv_sems(k, a, 1, d, 1), outer_next[d])
                send(line, line, sib_send.at[k, a, 1 + d], sib_recv.at[k, a, 1 + d], sibling)

    def kve(k):
        for a, (buf, inner, outer, inner_next, outer_next, parts) in enumerate(kinds):
            source = lax.rem(outer + 2, 4)
            for d in range(2):
                part = buf.at[k, core, source, pl.ds(2 * d, 2)]
                arrived(part, *kv_sems(k, a, 1, d, 1), outer_next[d])
            line = buf.at[k, core, source]
            send(line, line, sib_send.at[k, a, 3], sib_recv.at[k, a, 3], sibling)

    def kvf(k):
        for a, (buf, inner, outer, inner_next, outer_next, parts) in enumerate(kinds):
            for i, shift in enumerate((0, 3, 1, 2)):
                line = buf.at[k, 1 - core, lax.rem(outer + shift, 4)]
                arrived(line, sib_send.at[k, a, i], sib_recv.at[k, a, i], sibling)

    def absorb(r, j, g, edge):
        keys, bias, values = [], [], []
        xx = lax.div(g, 2)
        place = lax.rem(ctx, 4)
        for i in range(4):
            yy = lax.rem(g, 2) * 2 + i // 2
            keys.append(kt[j, i % 2, yy, xx, 0:HD, :])
            row = kt[j, i % 2, yy, xx, HD:K_TILE, :].astype(F32)[0:1, :]
            if edge and j != r:
                seen = i <= place if j < r else i < place
                row = row + jnp.where(seen, 0.0, NEG)
            bias.append(row)
            values.append(va[j, i % 2, xx, yy, :, :])
        scores = dot(qs[r], jnp.concatenate(keys, axis=1)) + jnp.concatenate(bias, axis=1)
        if edge and j == r:
            slot = lax.rem(lax.broadcasted_iota(jnp.int32, (Q_ROWS, CHUNK), 0), CHUNK)
            key = lax.broadcasted_iota(jnp.int32, (Q_ROWS, CHUNK), 1)
            ahead = key - slot
            pieces = []
            for i in range(4):
                limit = jnp.where(i < place, CHUNK, jnp.where(i == place, 0, -CHUNK))
                pieces.append(
                    jnp.where(ahead <= limit, scores[:, i * CHUNK : (i + 1) * CHUNK], NEG)
                )
            scores = jnp.concatenate(pieces, axis=1)
        before = m_s[r]
        after = jnp.maximum(before, jnp.max(scores, axis=1, keepdims=True))
        factor = jnp.exp2(before - after)
        probs = jnp.exp2(scores - jnp.concatenate([after] * 4, axis=1))
        m_s[r] = after
        l_s[r] = l_s[r] * factor + sum(probs[:, i * CHUNK : (i + 1) * CHUNK] for i in range(4))
        o_s[r] = o_s[r] * factor + dot(probs.astype(BF16), jnp.concatenate(values, axis=0))

    def attend(r, j):
        lax.fori_loop(0, lax.div(ctx, 4), lambda g, c: (absorb(r, j, g, False), c)[1], 0)
        absorb(r, j, lax.div(ctx, 4), True)

    def heads(r):
        if r == 0:
            weights[3].wait()
        mixed = (o_s[r] / jnp.sum(l_s[r], axis=1, keepdims=True)).astype(BF16)
        for h in range(GROUP):
            ho[r, :, h * HD : (h + 1) * HD] = mixed[h * CHUNK : (h + 1) * CHUNK, :]

    def term(r, block):
        block = lax.rem(block + NZ, NZ)
        columns = pl.ds(pl.multiple_of(block * FEATURES, FEATURES), FEATURES)
        return dot(ho[r], wo[:, columns])

    half = CHUNK // 2

    def rs(r, step):
        def rs_sems(d, hop):
            return rs_send.at[d, r, hop], rs_recv.at[d, r, hop]

        def rows(d, hop):
            return pl.ds(d * half, half) if hop == 0 else pl.ds(0, CHUNK)

        if step == 1:
            product = term(r, t + 4).astype(BF16)
            for d in range(2):
                sb[d, r, 0, rows(d, 0)] = product[d * half : (d + 1) * half]
        elif step < 5:
            for d, sign in enumerate((1, -1)):
                product = term(r, t + sign * (5 - step))
                landed = rb.at[d, r, step - 2, rows(d, step - 2)]
                arrived(landed, *rs_sems(d, step - 2), z_next[d])
                if step == 2:
                    keep = product[(1 - d) * half : (2 - d) * half].astype(BF16)
                    sb[d, r, 1, rows(1 - d, 0)] = keep
                    add = product[d * half : (d + 1) * half] + landed[...].astype(F32)
                    sb[d, r, 1, rows(d, 0)] = add.astype(BF16)
                else:
                    sb[d, r, step - 1] = (product + landed[...].astype(F32)).astype(BF16)
        if step < 5:
            for d in range(2):
                src = sb.at[d, r, step - 1, rows(d, step - 1)]
                dst = rb.at[d, r, step - 1, rows(d, step - 1)]
                send(src, dst, *rs_sems(d, step - 1), z_next[d])
            return
        total = term(r, t)
        for d in range(2):
            landed = rb.at[d, r, 3]
            arrived(landed, *rs_sems(d, 3), z_next[d])
            total = total + landed[...].astype(F32)
        weight = jnp.transpose(jnp.broadcast_to(router_ref[r : r + 1, :], (CHUNK, CHUNK)))
        total = total * jnp.concatenate([weight] * 4, axis=1)
        slot = lax.broadcasted_iota(jnp.int32, (CHUNK, FEATURES), 0) + r * CHUNK
        out_ref[pl.ds(r * CHUNK, CHUNK)] = jnp.where(slot < count, total, 0.0).astype(BF16)

    steps = {"kva": kva, "kvb": kvb, "kvc": kvc, "kvd": kvd, "kve": kve, "kvf": kvf}
    for event in SCHEDULE:
        if event == "own":
            own()
        elif event[:2] == "zs":
            z_start(int(event[2]), int(event[3]) + 1)
        elif event[0] == "z":
            z_step(int(event[1]), int(event[2]))
        elif event[:3] == "fin":
            finish(int(event[3]))
        elif event[:2] == "kv":
            steps[event[:3]](int(event[3]))
        elif event[:2] == "at":
            attend(int(event[2]), int(event[3]))
        elif event[:2] == "ho":
            heads(int(event[2]))
        else:
            rs(int(event[2]), int(event[3]))
    for copy in sends:
        copy.wait_send()


def body(routed_x, norm_gain, w_query, w_key, w_value, w_out, positions, counts, router_weight):
    vmem = pl.BlockSpec(memory_space=pltpu.VMEM)
    hbm = pl.BlockSpec(memory_space=pl.ANY)
    smem = pl.BlockSpec(memory_space=pltpu.SMEM)
    return pl.pallas_call(
        kernel,
        out_shape=jax.ShapeDtypeStruct((ROWS, FEATURES), BF16),
        in_specs=[vmem, vmem, hbm, hbm, hbm, hbm, smem, vmem],
        out_specs=vmem,
        scratch_shapes=[
            pltpu.VMEM((NZ, ROWS, FEATURES), BF16),
            pltpu.VMEM((NZ * FEATURES, GROUP * HD), BF16),
            pltpu.VMEM((NZ * FEATURES, 2 * HD), BF16),
            pltpu.VMEM((GROUP * HD, NZ * FEATURES), BF16),
            pltpu.VMEM((ROWS, GROUP * HD), F32),
            pltpu.VMEM((ROWS, 2 * HD), F32),
            pltpu.VMEM((ROWS, 128), F32),
            pltpu.VMEM((CHUNKS, Q_ROWS, HD), BF16),
            pltpu.VMEM((CHUNKS, 2, NY, NX, K_TILE, CHUNK), BF16),
            pltpu.VMEM((CHUNKS, 2, NX, NY, CHUNK, HD), BF16),
            pltpu.VMEM((CHUNKS, Q_ROWS, 128), F32),
            pltpu.VMEM((CHUNKS, Q_ROWS, 128), F32),
            pltpu.VMEM((CHUNKS, Q_ROWS, HD), F32),
            pltpu.VMEM((CHUNKS, CHUNK, GROUP * HD), BF16),
            pltpu.VMEM((2, CHUNKS, 4, CHUNK, FEATURES), BF16),
            pltpu.VMEM((2, CHUNKS, 4, CHUNK, FEATURES), BF16),
            pltpu.SemaphoreType.DMA((4,)),
            pltpu.SemaphoreType.DMA((2, CHUNKS, 4)),
            pltpu.SemaphoreType.DMA((2, CHUNKS, 4)),
            pltpu.SemaphoreType.DMA((CHUNKS, 2, 2, 2, 2)),
            pltpu.SemaphoreType.DMA((CHUNKS, 2, 2, 2, 2)),
            pltpu.SemaphoreType.DMA((CHUNKS, 2, 4)),
            pltpu.SemaphoreType.DMA((CHUNKS, 2, 4)),
            pltpu.SemaphoreType.DMA((2, CHUNKS, 4)),
            pltpu.SemaphoreType.DMA((2, CHUNKS, 4)),
        ],
        compiler_params=pltpu.CompilerParams(
            collective_id=0, has_side_effects=True, vmem_limit_bytes=56 * 1024 * 1024
        ),
    )(
        routed_x,
        norm_gain.reshape(NZ, 1, FEATURES),
        w_query,
        w_key,
        w_value,
        w_out,
        counts,
        router_weight.reshape(CHUNKS, CHUNK),
    )


def solution(mesh):
    return jax.shard_map(
        body,
        mesh=mesh,
        in_specs=(
            P("ctx", "tp"),
            P(),
            P(None, "tp"),
            P(None, "tp"),
            P(None, "tp"),
            P("tp", None),
            P("ctx"),
            P("ctx"),
            P("ctx"),
        ),
        out_specs=P("ctx", "tp"),
        check_vma=False,
    )
```

```python
import jax
import jax.numpy as jnp
from jax import lax
from jax.experimental import pallas as pl
from jax.experimental.pallas import tpu as pltpu
from jax.sharding import PartitionSpec as P

HD = 128
GROUP = 4
ROWS = 384
CHUNK = 128
CHUNKS = 3
FEATURES = 512
Q_ROWS = GROUP * CHUNK
SHARDS = 8
K_TILE = HD + 16
NX, NY, NZ = 4, 4, 8
NEG = -1e30
LOG2E = 1.4426950408889634
BF16 = jnp.bfloat16
F32 = jnp.float32

PIECES = ((0, 128, 0), (128, 64, 1), (192, 64, 1))
PIECES += ((256, 32, 2), (288, 32, 2), (320, 32, 2), (352, 32, 2))
SCHEDULE = (
    "zs0 zs1 zs2 own", "z01 pj01 z11 z21", "pj11 z02 pj02 z12", "z22 pj12 z03 pj03",
    "z13 zs3 z23 pj13", "zs4 zs5 zs6 z04", "pj04 fin0 kva0 fq0", "z14 z31 z24 pj14",
    "fin1 kva1 fq1 z41", "z51 z61 pj21 z32", "z42 kvb0 z52 z62", "pj22 z33 kvb1 z43",
    "z53 z63 pj23 z34", "z44 z54 z64 pk24", "fin2 kva2 pq24 fq2", "gq kvc0 kvd0 at00",
    "kvb2 kvc1 gw al1", "kvd1 ap1 kvc2 al2", "kvd2 at32 gs at02", "ho0 rs01 tma0 at12",
    "rs02 ho1 rs11 tma1", "tmb0 at22 gr ho2", "rs21 tma2 rs12 rs03", "tmb1 rs22 rs13 rs04",
    "tmb2 rs23 rs14 rs05", "rs24 rs15 rs25",
)


def dot(a, b):
    return jnp.dot(a, b, preferred_element_type=F32)


def kernel(
    x_hbm, gain_hbm, wq_hbm, wk_hbm, wv_hbm, wo_hbm, count_ref, router_hbm, out_hbm,
    xg, gain_ref, router_ref, out_ref, wq, wkv, wo, acc_q, acc_kv, ssq, qs, kt, va, m_s, l_s, o_s, ho, tm, sb, rb,
    w_sem, z_send, z_recv, kv_send, kv_recv, sib_send, sib_recv, rs_send, rs_recv,
    guest_sem, out_sem,
):
    ctx = lax.axis_index("ctx")
    t = lax.axis_index("tp")
    core = lax.rem(ctx, 2)
    y = lax.rem(lax.div(ctx, 2), NY)
    x = lax.div(ctx, 2 * NY)

    def at(xx, yy, cc, tt):
        return ((lax.rem(xx, NX) * NY + lax.rem(yy, NY)) * 2 + cc, lax.rem(tt, NZ))

    z_next = (at(x, y, core, t + 1), at(x, y, core, t + NZ - 1))
    x_line = tuple(at(x + i, y, core, t) for i in (1, 3, 2))
    y_line = tuple(at(x, y + i, core, t) for i in (1, 3, 2))
    sibling = at(x, y, 1 - core, t)
    count = count_ref[0]

    weights = [
        pltpu.make_async_copy(wq_hbm, wq, w_sem.at[0]),
        pltpu.make_async_copy(wk_hbm, wkv.at[:, pl.ds(0, HD)], w_sem.at[1]),
        pltpu.make_async_copy(wv_hbm, wkv.at[:, pl.ds(HD, HD)], w_sem.at[2]),
        pltpu.make_async_copy(gain_hbm, gain_ref, w_sem.at[3]),
        pltpu.make_async_copy(x_hbm, xg.at[t], w_sem.at[4]),
        pltpu.make_async_copy(wo_hbm, wo, w_sem.at[5]),
        pltpu.make_async_copy(router_hbm, router_ref, w_sem.at[6]),
    ]
    for copy in weights:
        copy.start()

    barrier = pltpu.get_barrier_semaphore()
    peers = z_next + x_line + y_line + (sibling,)
    for peer in peers:
        pl.semaphore_signal(barrier, inc=1, device_id=peer, device_id_type=pl.DeviceIdType.MESH)
    pl.semaphore_wait(barrier, len(peers))

    sends = []

    def remote(src, dst, send_sem, recv_sem, device):
        return pltpu.make_async_remote_copy(
            src_ref=src, dst_ref=dst, send_sem=send_sem, recv_sem=recv_sem,
            device_id=device, device_id_type=pl.DeviceIdType.MESH,
        )

    def send(src, dst, send_sem, recv_sem, device):
        copy = remote(src, dst, send_sem, recv_sem, device)
        copy.start()
        sends.append(copy)

    def arrived(dst, send_sem, recv_sem, device):
        remote(dst, dst, send_sem, recv_sem, device).wait_recv()

    def z_rows(d, p, h):
        first, size, chunk = PIECES[p]
        if h < 4:
            return pl.ds(first, size)
        return pl.ds(first + d * (size // 2), size // 2)

    def z_start(p, h):
        for d, sign in enumerate((1, -1)):
            block = lax.rem(t - sign * (h - 1) + NZ, NZ)
            dst = xg.at[block, z_rows(d, p, h)]
            src = x_hbm.at[z_rows(d, p, h)] if h == 1 else dst
            send(src, dst, z_send.at[d, p, h - 1], z_recv.at[d, p, h - 1], z_next[d])

    def project(block, rows, keys, queries):
        widened = xg[block, rows].astype(F32)
        scaled = (widened * gain_ref[block]).astype(BF16)
        features = pl.ds(pl.multiple_of(block * FEATURES, FEATURES), FEATURES)
        if keys:
            squares = widened * widened
            ssq[rows] += sum(squares[:, i * 128 : (i + 1) * 128] for i in range(FEATURES // 128))
            acc_kv[rows] += dot(scaled, wkv[features])
        if queries:
            acc_q[rows] += dot(scaled, wq[features])

    def z_step(p, h):
        for d, sign in enumerate((1, -1)):
            block = lax.rem(t - sign * h + NZ, NZ)
            arrived(
                xg.at[block, z_rows(d, p, h)], z_send.at[d, p, h - 1], z_recv.at[d, p, h - 1], z_next[d]
            )
        if h < 4:
            z_start(p, h + 1)

    def z_project(k, h, keys=True, queries=True):
        for sign in (1, -1) if h < 4 else (1,):
            block = lax.rem(t - sign * h + NZ, NZ)
            project(block, pl.ds(k * CHUNK, CHUNK), keys, queries)

    def own():
        for copy in weights[:5]:
            copy.wait()
        ssq[...] = jnp.zeros_like(ssq)
        acc_q[...] = jnp.zeros_like(acc_q)
        acc_kv[...] = jnp.zeros_like(acc_kv)
        m_s[...] = jnp.full_like(m_s, NEG)
        l_s[...] = jnp.zeros_like(l_s)
        o_s[...] = jnp.zeros_like(o_s)
        project(t, pl.ds(0, ROWS), True, True)

    def row_scale(rows):
        mean = jnp.sum(ssq[rows], axis=1, keepdims=True) * (1.0 / (NZ * FEATURES))
        return lax.rsqrt(mean + 1e-05)

    def finish_queries(k):
        rows = pl.ds(k * CHUNK, CHUNK)
        query = (acc_q[rows] * (row_scale(rows) * (HD**-0.5 * LOG2E))).astype(BF16)
        for h in range(GROUP):
            qs[k, h * CHUNK : (h + 1) * CHUNK, :] = query[:, h * HD : (h + 1) * HD]

    def finish_keys(k):
        rows = pl.ds(k * CHUNK, CHUNK)
        pair = acc_kv[rows] * row_scale(rows)
        kt[k, core, y, x, 0:HD, :] = jnp.transpose(pair[:, :HD]).astype(BF16)
        slot = lax.broadcasted_iota(jnp.int32, (16, CHUNK), 1) + k * CHUNK
        kt[k, core, y, x, HD:K_TILE, :] = jnp.where(slot < count, 0.0, NEG).astype(BF16)
        va[k, core, x, y, :, :] = pair[:, HD:].astype(BF16)

    kinds = ((kt, x, y, x_line, y_line), (va, y, x, y_line, x_line))

    def kv_sems(k, a, phase, i):
        return kv_send.at[k, a, phase, i], kv_recv.at[k, a, phase, i]

    def kva(k):
        for a, (buf, inner, outer, inner_line, outer_line) in enumerate(kinds):
            tile = buf.at[k, core, outer, inner]
            for i in range(3):
                send(tile, tile, *kv_sems(k, a, 0, i), inner_line[i])

    def kvb(k):
        for a, (buf, inner, outer, inner_line, outer_line) in enumerate(kinds):
            for i in range(3):
                tile = buf.at[k, core, outer, lax.rem(inner + (3, 1, 2)[i], 4)]
                arrived(tile, *kv_sems(k, a, 0, i), inner_line[i])
            line = buf.at[k, core, outer]
            for i in range(3):
                send(line, line, *kv_sems(k, a, 1, i), outer_line[i])
            send(line, line, sib_send.at[k, a, 3], sib_recv.at[k, a, 3], sibling)

    def kvc(k):
        for i in range(3):
            for a, (buf, inner, outer, inner_line, outer_line) in enumerate(kinds):
                line = buf.at[k, core, lax.rem(outer + (3, 1, 2)[i], 4)]
                arrived(line, *kv_sems(k, a, 1, i), outer_line[i])
                send(line, line, sib_send.at[k, a, i], sib_recv.at[k, a, i], sibling)

    def kvd(k):
        for a, (buf, inner, outer, inner_line, outer_line) in enumerate(kinds):
            for i in range(4):
                line = buf.at[k, 1 - core, lax.rem(outer + (3, 1, 2, 0)[i], 4)]
                arrived(line, sib_send.at[k, a, i], sib_recv.at[k, a, i], sibling)

    place = lax.rem(ctx, SHARDS)
    host, lender = x == 0, x == NX - 1

    def absorb(r, chunk, j, g, last, pair=False):
        count_rows = 2 * Q_ROWS if pair else Q_ROWS
        slot = lax.rem(lax.broadcasted_iota(jnp.int32, (count_rows, CHUNK), 0), CHUNK)
        if pair:
            half_rows = lax.broadcasted_iota(jnp.int32, (count_rows, CHUNK), 0)
            slot = jnp.where(half_rows < Q_ROWS, slot, slot + CHUNK)
        slot = slot.astype(F32)

        def rows_of(ref):
            return ref[0:2].reshape(count_rows, HD) if pair else ref[r]

        def put(ref, value):
            if pair:
                ref[0:2] = value.reshape(2, Q_ROWS, HD)
            else:
                ref[r] = value

        column = lax.broadcasted_iota(jnp.int32, (1, CHUNK), 1)
        keys, first, values = [], [], []
        own_limit = jnp.where(j < chunk, CHUNK, jnp.where(j == chunk, 0, -CHUNK))
        if pair:
            own_limit = -j * CHUNK
        for i in range(SHARDS):
            keys.append(kt[j, i % 2, i // 2, g, 0:HD, :])
            mask = kt[j, i % 2, i // 2, g, HD:K_TILE, :].astype(F32)[0:1, :]
            limit = jnp.where(i < place, ROWS, jnp.where(i == place, own_limit, -ROWS))
            limit = jnp.where(g < last, ROWS, limit)
            first.append(jnp.where(mask < 0.0, 1e9, (column - limit).astype(F32)))
            values.append(va[j, i % 2, g, i // 2, :, :])
        scores = dot(rows_of(qs), jnp.concatenate(keys, axis=1))
        scores = [
            jnp.where(first[i] <= slot, scores[:, i * CHUNK : (i + 1) * CHUNK], NEG)
            for i in range(SHARDS)
        ]
        scores = jnp.concatenate(scores, axis=1)
        before = rows_of(m_s)
        after = jnp.maximum(before, jnp.max(scores, axis=1, keepdims=True))
        factor = jnp.exp2(before - after)
        probs = jnp.exp2(scores - jnp.concatenate([after] * SHARDS, axis=1))
        put(m_s, after)
        lanes = sum(probs[:, i * CHUNK : (i + 1) * CHUNK] for i in range(SHARDS))
        put(l_s, rows_of(l_s) * factor + lanes)
        mixed = dot(probs.astype(BF16), jnp.concatenate(values, axis=0))
        put(o_s, rows_of(o_s) * factor + mixed)

    def attend(r, j):
        guest = jnp.int32(r) == 3
        lent = (jnp.int32(r) == 2) & lender
        last = jnp.where(guest, NX - 1, x)
        groups = jnp.where(guest, jnp.where(host, NX, 0), jnp.where(lent, 0, x + 1))
        chunk = jnp.minimum(jnp.int32(r), 2)

        @pl.loop(0, groups)
        def _(g):
            absorb(r, chunk, jnp.int32(j), g, last)

    def attend_pair(j):
        pl.loop(0, x + 1)(lambda g: absorb(0, 0, jnp.int32(j), g, x, pair=True))

    def attend_many(first):
        if first == 1:
            pl.loop(1, 4)(lambda r: attend(r, 0))
        else:
            pl.loop(2, 4)(lambda r: attend(r, 1))

    def guest_copy(back):
        i = 1 if back else 0
        src = ho.at[3] if back else qs.at[2]
        dst = ho.at[2] if back else qs.at[3]
        return remote(src, dst, guest_sem.at[i], guest_sem.at[2 + i], x_line[i])

    def guest_query():
        pl.when(lender)(lambda: guest_copy(False).start())

    def guest_wait():
        pl.when(host)(lambda: guest_copy(False).wait_recv())

    def guest_send():
        @pl.when(host)
        def _():
            mix(3)
            guest_copy(True).start()

    def guest_return():
        pl.when(lender)(lambda: guest_copy(True).wait_recv())

    def mix(r):
        mixed = (o_s[r] / jnp.sum(l_s[r], axis=1, keepdims=True)).astype(BF16)
        for h in range(GROUP):
            ho[r, :, h * HD : (h + 1) * HD] = mixed[h * CHUNK : (h + 1) * CHUNK, :]

    def heads(r):
        if r == 0:
            weights[5].wait()
            weights[6].wait()
        if r == 2:
            pl.when(jnp.logical_not(lender))(lambda: mix(2))
        else:
            mix(r)

    def term(r, block):
        block = lax.rem(block + NZ, NZ)
        columns = pl.ds(pl.multiple_of(block * FEATURES, FEATURES), FEATURES)
        return dot(ho[r], wo[:, columns])

    half = CHUNK // 2

    def result_copy(r):
        return pltpu.make_async_copy(
            out_ref.at[r], out_hbm.at[pl.ds(r * CHUNK, CHUNK)], out_sem.at[r]
        )

    def terms(r, shifts):
        for shift in shifts:
            tm[r, shift + 3] = term(r, t + shift)

    def rs(r, step):
        def rs_sems(d, hop):
            return rs_send.at[d, r, hop], rs_recv.at[d, r, hop]

        def rows(d, hop):
            return pl.ds(d * half, half) if hop == 0 else pl.ds(0, CHUNK)

        if step == 1:
            product = term(r, t + 4).astype(BF16)
            for d in range(2):
                sb[d, r, 0, rows(d, 0)] = product[d * half : (d + 1) * half]
        for d, sign in enumerate((1, -1)):
            if step == 5:
                break
            if step > 1:
                product = tm.at[r, 3 + sign * (5 - step)]
                landed = rb.at[d, r, step - 2, rows(d, step - 2)]
                arrived(landed, *rs_sems(d, step - 2), z_next[d])
                if step == 2:
                    sb[d, r, 1, rows(1 - d, 0)] = product[rows(1 - d, 0)].astype(BF16)
                add = product[rows(d, step - 2)] + landed[...].astype(F32)
                sb[d, r, step - 1, rows(d, step - 2)] = add.astype(BF16)
            src = sb.at[d, r, step - 1, rows(d, step - 1)]
            dst = rb.at[d, r, step - 1, rows(d, step - 1)]
            send(src, dst, *rs_sems(d, step - 1), z_next[d])
        if step < 5:
            return
        total = tm[r, 3]
        for d in range(2):
            landed = rb.at[d, r, 3]
            arrived(landed, *rs_sems(d, 3), z_next[d])
            total = total + landed[...].astype(F32)
        weight = jnp.transpose(jnp.broadcast_to(router_ref[r : r + 1, :], (CHUNK, CHUNK)))
        total = total * jnp.concatenate([weight] * 4, axis=1)
        slot = lax.broadcasted_iota(jnp.int32, (CHUNK, FEATURES), 0) + r * CHUNK
        out_ref[r] = jnp.where(slot < count, total, 0.0).astype(BF16)
        result_copy(r).start()

    steps = {"zs": lambda p: z_start(p, 1), "z": z_step, "pj": z_project}
    steps |= {"pk": lambda k, h: z_project(k, h, queries=False), "fin": finish_keys}
    steps |= {"pq": lambda k, h: z_project(k, h, keys=False), "fq": finish_queries}
    steps |= {"kva": kva, "kvb": kvb, "kvc": kvc, "kvd": kvd}
    steps |= {"gq": guest_query, "gw": guest_wait, "gs": guest_send, "gr": guest_return}
    steps |= {"al": attend_many, "ap": attend_pair, "own": own, "at": attend, "ho": heads, "tma": lambda r: terms(r, (3, -3)), "tmb": lambda r: terms(r, (2, -2, 1, -1, 0)), "rs": rs}
    for event in " ".join(SCHEDULE).split():
        name = event.rstrip("0123456789")
        steps[name](*map(int, event[len(name) :]))
    for copy in sends:
        copy.wait_send()
    for r in range(CHUNKS):
        result_copy(r).wait()
    pl.when(lender)(lambda: guest_copy(False).wait_send())
    pl.when(host)(lambda: guest_copy(True).wait_send())


def body(routed_x, norm_gain, w_query, w_key, w_value, w_out, positions, counts, router_weight):
    hbm = pl.BlockSpec(memory_space=pl.ANY)
    smem = pl.BlockSpec(memory_space=pltpu.SMEM)
    return pl.pallas_call(
        kernel,
        out_shape=jax.ShapeDtypeStruct((ROWS, FEATURES), BF16),
        in_specs=[hbm] * 6 + [smem, hbm],
        out_specs=hbm,
        scratch_shapes=[
            pltpu.VMEM((NZ, ROWS, FEATURES), BF16),
            pltpu.VMEM((NZ, 1, FEATURES), F32),
            pltpu.VMEM((CHUNKS, CHUNK), F32),
            pltpu.VMEM((CHUNKS, CHUNK, FEATURES), BF16),
            pltpu.VMEM((NZ * FEATURES, GROUP * HD), BF16),
            pltpu.VMEM((NZ * FEATURES, 2 * HD), BF16),
            pltpu.VMEM((GROUP * HD, NZ * FEATURES), BF16),
            pltpu.VMEM((ROWS, GROUP * HD), F32),
            pltpu.VMEM((ROWS, 2 * HD), F32),
            pltpu.VMEM((ROWS, 128), F32),
            pltpu.VMEM((CHUNKS + 1, Q_ROWS, HD), BF16),
            pltpu.VMEM((CHUNKS, 2, NY, NX, K_TILE, CHUNK), BF16),
            pltpu.VMEM((CHUNKS, 2, NX, NY, CHUNK, HD), BF16),
            pltpu.VMEM((CHUNKS + 1, Q_ROWS, 128), F32),
            pltpu.VMEM((CHUNKS + 1, Q_ROWS, 128), F32),
            pltpu.VMEM((CHUNKS + 1, Q_ROWS, HD), F32),
            pltpu.VMEM((CHUNKS + 1, CHUNK, GROUP * HD), BF16),
            pltpu.VMEM((CHUNKS, 7, CHUNK, FEATURES), F32),
            pltpu.VMEM((2, CHUNKS, 4, CHUNK, FEATURES), BF16),
            pltpu.VMEM((2, CHUNKS, 4, CHUNK, FEATURES), BF16),
            pltpu.SemaphoreType.DMA((7,)),
            pltpu.SemaphoreType.DMA((2, len(PIECES), 4)),
            pltpu.SemaphoreType.DMA((2, len(PIECES), 4)),
            pltpu.SemaphoreType.DMA((CHUNKS, 2, 2, 3)),
            pltpu.SemaphoreType.DMA((CHUNKS, 2, 2, 3)),
            pltpu.SemaphoreType.DMA((CHUNKS, 2, 4)),
            pltpu.SemaphoreType.DMA((CHUNKS, 2, 4)),
            pltpu.SemaphoreType.DMA((2, CHUNKS, 4)),
            pltpu.SemaphoreType.DMA((2, CHUNKS, 4)),
            pltpu.SemaphoreType.DMA((4,)),
            pltpu.SemaphoreType.DMA((CHUNKS,)),
        ],
        compiler_params=pltpu.CompilerParams(
            collective_id=0, has_side_effects=True, vmem_limit_bytes=56 * 1024 * 1024
        ),
    )(
        routed_x,
        norm_gain.reshape(NZ, 1, FEATURES),
        w_query,
        w_key,
        w_value,
        w_out,
        counts,
        router_weight.reshape(CHUNKS, CHUNK),
    )


def solution(mesh):
    return jax.shard_map(
        body,
        mesh=mesh,
        in_specs=(
            P("ctx", "tp"),
            P(),
            P(None, "tp"),
            P(None, "tp"),
            P(None, "tp"),
            P("tp", None),
            P("ctx"),
            P("ctx"),
            P("ctx"),
        ),
        out_specs=P("ctx", "tp"),
        check_vma=False,
    )
```

```python
import jax
import jax.numpy as jnp
from jax import lax
from jax.experimental import pallas as pl
from jax.experimental.pallas import tpu as pltpu
from jax.sharding import PartitionSpec as P

HD = 128
GROUP = 4
ROWS = 384
CHUNK = 128
CHUNKS = 3
FEATURES = 512
Q_ROWS = GROUP * CHUNK
SHARDS = 8
K_TILE = HD + 16
NX, NY, NZ = 4, 4, 8
NEG = -1e30
LOG2E = 1.4426950408889634
BF16 = jnp.bfloat16
F32 = jnp.float32

PIECES = ((0, 128, 0), (128, 64, 1), (192, 64, 1))
PIECES += ((256, 32, 2), (288, 32, 2), (320, 32, 2), (352, 32, 2))
SCHEDULE = (
    "zs0 zs1 zs2 own", "z01 pj01 z11 z21", "pj11 z02 pj02 z12", "z22 pj12 z03 pj03",
    "z13 zs3 z23 pj13", "zs4 zs5 zs6 z04", "pj04 fin0 kva0 fq0", "z14 z31 z24 pj14",
    "fin1 kva1 fq1 z41", "z51 z61 pj21 kvb0", "z32 z42 z52 z62", "pj22 z33 kvb1 z43",
    "z53 z63 pj23 z34", "z44 z54 z64 pk24", "fin2 kva2 pq24 fq2", "gq kvc0 kvd0 at00",
    "kvb2 kvc1 gw al0", "kvd1 ap1 kvc2 al1", "kvd2 at02 ho0 rs01", "tma0 at32 gs at12",
    "rs02 ho1 rs11 tma1", "tmb0 at22 gr ho2", "rs21 tma2 rs12 rs03", "tmb1 rs22 rs13 rs04",
    "tmb2 rs23 rs14 rs05", "rs24 rs15 rs25",
)


def dot(a, b):
    return jnp.dot(a, b, preferred_element_type=F32)


def kernel(
    x_hbm, gain_hbm, wq_hbm, wk_hbm, wv_hbm, wo_hbm, count_ref, router_hbm, out_hbm,
    xg, gain_ref, router_ref, out_ref, wq, wkv, wo, acc_q, acc_kv, ssq, qs, kt, va, m_s, l_s, o_s, ho, tm, sb, rb,
    w_sem, z_send, z_recv, kv_send, kv_recv, sib_send, sib_recv, rs_send, rs_recv,
    guest_sem, out_sem,
):
    ctx = lax.axis_index("ctx")
    t = lax.axis_index("tp")
    core = lax.rem(ctx, 2)
    y = lax.rem(lax.div(ctx, 2), NY)
    x = lax.div(ctx, 2 * NY)

    def at(xx, yy, cc, tt):
        return ((lax.rem(xx, NX) * NY + lax.rem(yy, NY)) * 2 + cc, lax.rem(tt, NZ))

    z_next = (at(x, y, core, t + 1), at(x, y, core, t + NZ - 1))
    x_line = tuple(at(x + i, y, core, t) for i in (1, 3, 2))
    y_line = tuple(at(x, y + i, core, t) for i in (1, 3, 2))
    sibling = at(x, y, 1 - core, t)
    count = count_ref[0]

    weights = [
        pltpu.make_async_copy(wq_hbm, wq, w_sem.at[0]),
        pltpu.make_async_copy(wk_hbm, wkv.at[:, pl.ds(0, HD)], w_sem.at[1]),
        pltpu.make_async_copy(wv_hbm, wkv.at[:, pl.ds(HD, HD)], w_sem.at[2]),
        pltpu.make_async_copy(gain_hbm, gain_ref, w_sem.at[3]),
        pltpu.make_async_copy(x_hbm, xg.at[t], w_sem.at[4]),
        pltpu.make_async_copy(wo_hbm, wo, w_sem.at[5]),
        pltpu.make_async_copy(router_hbm, router_ref, w_sem.at[6]),
    ]
    for copy in weights:
        copy.start()

    barrier = pltpu.get_barrier_semaphore()
    peers = z_next + x_line + y_line + (sibling,)
    for peer in peers:
        pl.semaphore_signal(barrier, inc=1, device_id=peer, device_id_type=pl.DeviceIdType.MESH)
    pl.semaphore_wait(barrier, len(peers))

    sends = []

    def remote(src, dst, send_sem, recv_sem, device):
        return pltpu.make_async_remote_copy(
            src_ref=src, dst_ref=dst, send_sem=send_sem, recv_sem=recv_sem,
            device_id=device, device_id_type=pl.DeviceIdType.MESH,
        )

    def send(src, dst, send_sem, recv_sem, device):
        copy = remote(src, dst, send_sem, recv_sem, device)
        copy.start()
        sends.append(copy)

    def arrived(dst, send_sem, recv_sem, device):
        remote(dst, dst, send_sem, recv_sem, device).wait_recv()

    def z_rows(d, p, h):
        first, size, chunk = PIECES[p]
        if h < 4:
            return pl.ds(first, size)
        return pl.ds(first + d * (size // 2), size // 2)

    def z_start(p, h):
        for d, sign in enumerate((1, -1)):
            block = lax.rem(t - sign * (h - 1) + NZ, NZ)
            dst = xg.at[block, z_rows(d, p, h)]
            src = x_hbm.at[z_rows(d, p, h)] if h == 1 else dst
            send(src, dst, z_send.at[d, p, h - 1], z_recv.at[d, p, h - 1], z_next[d])

    def project(block, rows, keys, queries):
        widened = xg[block, rows].astype(F32)
        scaled = (widened * gain_ref[block]).astype(BF16)
        features = pl.ds(pl.multiple_of(block * FEATURES, FEATURES), FEATURES)
        if keys:
            squares = widened * widened
            ssq[rows] += sum(squares[:, i * 128 : (i + 1) * 128] for i in range(FEATURES // 128))
            acc_kv[rows] += dot(scaled, wkv[features])
        if queries:
            acc_q[rows] += dot(scaled, wq[features])

    def z_step(p, h):
        for d, sign in enumerate((1, -1)):
            block = lax.rem(t - sign * h + NZ, NZ)
            arrived(
                xg.at[block, z_rows(d, p, h)], z_send.at[d, p, h - 1], z_recv.at[d, p, h - 1], z_next[d]
            )
        if h < 4:
            z_start(p, h + 1)

    def z_project(k, h, keys=True, queries=True):
        for sign in (1, -1) if h < 4 else (1,):
            block = lax.rem(t - sign * h + NZ, NZ)
            project(block, pl.ds(k * CHUNK, CHUNK), keys, queries)

    def own():
        for copy in weights[:5]:
            copy.wait()
        ssq[...] = jnp.zeros_like(ssq)
        acc_q[...] = jnp.zeros_like(acc_q)
        acc_kv[...] = jnp.zeros_like(acc_kv)
        m_s[...] = jnp.full_like(m_s, NEG)
        l_s[...] = jnp.zeros_like(l_s)
        o_s[...] = jnp.zeros_like(o_s)
        project(t, pl.ds(0, ROWS), True, True)

    def row_scale(rows):
        mean = jnp.sum(ssq[rows], axis=1, keepdims=True) * (1.0 / (NZ * FEATURES))
        return lax.rsqrt(mean + 1e-05)

    def finish_queries(k):
        rows = pl.ds(k * CHUNK, CHUNK)
        query = (acc_q[rows] * (row_scale(rows) * (HD**-0.5 * LOG2E))).astype(BF16)
        for h in range(GROUP):
            qs[k, h * CHUNK : (h + 1) * CHUNK, :] = query[:, h * HD : (h + 1) * HD]

    def finish_keys(k):
        rows = pl.ds(k * CHUNK, CHUNK)
        pair = acc_kv[rows] * row_scale(rows)
        kt[k, core, y, x, 0:HD, :] = jnp.transpose(pair[:, :HD]).astype(BF16)
        slot = lax.broadcasted_iota(jnp.int32, (16, CHUNK), 1) + k * CHUNK
        kt[k, core, y, x, HD:K_TILE, :] = jnp.where(slot < count, 0.0, NEG).astype(BF16)
        va[k, core, x, y, :, :] = pair[:, HD:].astype(BF16)

    kinds = ((kt, x, y, x_line, y_line), (va, y, x, y_line, x_line))

    def kv_sems(k, a, phase, i):
        return kv_send.at[k, a, phase, i], kv_recv.at[k, a, phase, i]

    def kva(k):
        for a, (buf, inner, outer, inner_line, outer_line) in enumerate(kinds):
            tile = buf.at[k, core, outer, inner]
            for i in range(3):
                send(tile, tile, *kv_sems(k, a, 0, i), inner_line[i])

    def kvb(k):
        for a, (buf, inner, outer, inner_line, outer_line) in enumerate(kinds):
            for i in range(3):
                tile = buf.at[k, core, outer, lax.rem(inner + (3, 1, 2)[i], 4)]
                arrived(tile, *kv_sems(k, a, 0, i), inner_line[i])
            line = buf.at[k, core, outer]
            for i in range(3):
                send(line, line, *kv_sems(k, a, 1, i), outer_line[i])
            send(line, line, sib_send.at[k, a, 3], sib_recv.at[k, a, 3], sibling)

    def kvc(k):
        for i in range(3):
            for a, (buf, inner, outer, inner_line, outer_line) in enumerate(kinds):
                line = buf.at[k, core, lax.rem(outer + (3, 1, 2)[i], 4)]
                arrived(line, *kv_sems(k, a, 1, i), outer_line[i])
                send(line, line, sib_send.at[k, a, i], sib_recv.at[k, a, i], sibling)

    def kvd(k):
        for a, (buf, inner, outer, inner_line, outer_line) in enumerate(kinds):
            for i in range(4):
                line = buf.at[k, 1 - core, lax.rem(outer + (3, 1, 2, 0)[i], 4)]
                arrived(line, sib_send.at[k, a, i], sib_recv.at[k, a, i], sibling)

    place = lax.rem(ctx, SHARDS)
    host, lender = x == 0, x == NX - 1

    def absorb(r, chunk, j, g, last, pair=False):
        count_rows = 2 * Q_ROWS if pair else Q_ROWS
        slot = lax.rem(lax.broadcasted_iota(jnp.int32, (count_rows, CHUNK), 0), CHUNK)
        if pair:
            half_rows = lax.broadcasted_iota(jnp.int32, (count_rows, CHUNK), 0)
            slot = jnp.where(half_rows < Q_ROWS, slot, slot + CHUNK)
        slot = slot.astype(F32)

        def rows_of(ref):
            return ref[0:2].reshape(count_rows, HD) if pair else ref[r]

        def put(ref, value):
            if pair:
                ref[0:2] = value.reshape(2, Q_ROWS, HD)
            else:
                ref[r] = value

        column = lax.broadcasted_iota(jnp.int32, (1, CHUNK), 1)
        keys, first, values = [], [], []
        own_limit = jnp.where(j < chunk, CHUNK, jnp.where(j == chunk, 0, -CHUNK))
        if pair:
            own_limit = -j * CHUNK
        for i in range(SHARDS):
            keys.append(kt[j, i % 2, i // 2, g, 0:HD, :])
            mask = kt[j, i % 2, i // 2, g, HD:K_TILE, :].astype(F32)[0:1, :]
            limit = jnp.where(i < place, ROWS, jnp.where(i == place, own_limit, -ROWS))
            limit = jnp.where(g < last, ROWS, limit)
            first.append(jnp.where(mask < 0.0, 1e9, (column - limit).astype(F32)))
            values.append(va[j, i % 2, g, i // 2, :, :])
        scores = dot(rows_of(qs), jnp.concatenate(keys, axis=1))
        scores = [
            jnp.where(first[i] <= slot, scores[:, i * CHUNK : (i + 1) * CHUNK], NEG)
            for i in range(SHARDS)
        ]
        scores = jnp.concatenate(scores, axis=1)
        before = rows_of(m_s)
        after = jnp.maximum(before, jnp.max(scores, axis=1, keepdims=True))
        factor = jnp.exp2(before - after)
        probs = jnp.exp2(scores - jnp.concatenate([after] * SHARDS, axis=1))
        put(m_s, after)
        lanes = sum(probs[:, i * CHUNK : (i + 1) * CHUNK] for i in range(SHARDS))
        put(l_s, rows_of(l_s) * factor + lanes)
        mixed = dot(probs.astype(BF16), jnp.concatenate(values, axis=0))
        put(o_s, rows_of(o_s) * factor + mixed)

    def attend(r, j):
        guest = jnp.int32(r) == 3
        lent = (jnp.int32(r) == 2) & lender
        last = jnp.where(guest, NX - 1, x)
        groups = jnp.where(guest, jnp.where(host, NX, 0), jnp.where(lent, 0, x + 1))
        chunk = jnp.minimum(jnp.int32(r), 2)

        pairs = lax.div(groups, 2)

        @pl.loop(0, pairs)
        def _(i):
            absorb(r, chunk, jnp.int32(j), 2 * i, last)
            absorb(r, chunk, jnp.int32(j), 2 * i + 1, last)

        @pl.loop(2 * pairs, groups)
        def _(g):
            absorb(r, chunk, jnp.int32(j), g, last)

    def attend_pair(j):
        pl.loop(0, x + 1)(lambda g: absorb(0, 0, jnp.int32(j), g, x, pair=True))

    def attend_many(j):
        pl.loop(1 + j, 4)(lambda r: attend(r, j))

    def guest_copy(back):
        i = 1 if back else 0
        src = ho.at[3] if back else qs.at[2]
        dst = ho.at[2] if back else qs.at[3]
        return remote(src, dst, guest_sem.at[i], guest_sem.at[2 + i], x_line[i])

    def guest_query():
        pl.when(lender)(lambda: guest_copy(False).start())

    def guest_wait():
        pl.when(host)(lambda: guest_copy(False).wait_recv())

    def guest_send():
        @pl.when(host)
        def _():
            mix(3)
            guest_copy(True).start()

    def guest_return():
        pl.when(lender)(lambda: guest_copy(True).wait_recv())

    def mix(r):
        mixed = (o_s[r] / jnp.sum(l_s[r], axis=1, keepdims=True)).astype(BF16)
        for h in range(GROUP):
            ho[r, :, h * HD : (h + 1) * HD] = mixed[h * CHUNK : (h + 1) * CHUNK, :]

    def heads(r):
        if r == 0:
            weights[5].wait()
            weights[6].wait()
        if r == 2:
            pl.when(jnp.logical_not(lender))(lambda: mix(2))
        else:
            mix(r)

    def term(r, block):
        block = lax.rem(block + NZ, NZ)
        columns = pl.ds(pl.multiple_of(block * FEATURES, FEATURES), FEATURES)
        return dot(ho[r], wo[:, columns])

    half = CHUNK // 2

    def result_copy(r):
        return pltpu.make_async_copy(
            out_ref.at[r], out_hbm.at[pl.ds(r * CHUNK, CHUNK)], out_sem.at[r]
        )

    def terms(r, shifts):
        for shift in shifts:
            tm[r, shift + 3] = term(r, t + shift)

    def rs(r, step):
        def rs_sems(d, hop):
            return rs_send.at[d, r, hop], rs_recv.at[d, r, hop]

        def rows(d, hop):
            return pl.ds(d * half, half) if hop == 0 else pl.ds(0, CHUNK)

        if step == 1:
            product = term(r, t + 4).astype(BF16)
            for d in range(2):
                sb[d, r, 0, rows(d, 0)] = product[d * half : (d + 1) * half]
        for d, sign in enumerate((1, -1)):
            if step == 5:
                break
            if step > 1:
                product = tm.at[r, 3 + sign * (5 - step)]
                landed = rb.at[d, r, step - 2, rows(d, step - 2)]
                arrived(landed, *rs_sems(d, step - 2), z_next[d])
                if step == 2:
                    sb[d, r, 1, rows(1 - d, 0)] = product[rows(1 - d, 0)].astype(BF16)
                add = product[rows(d, step - 2)] + landed[...].astype(F32)
                sb[d, r, step - 1, rows(d, step - 2)] = add.astype(BF16)
            src = sb.at[d, r, step - 1, rows(d, step - 1)]
            dst = rb.at[d, r, step - 1, rows(d, step - 1)]
            send(src, dst, *rs_sems(d, step - 1), z_next[d])
        if step < 5:
            return
        total = tm[r, 3]
        for d in range(2):
            landed = rb.at[d, r, 3]
            arrived(landed, *rs_sems(d, 3), z_next[d])
            total = total + landed[...].astype(F32)
        weight = jnp.transpose(jnp.broadcast_to(router_ref[r : r + 1, :], (CHUNK, CHUNK)))
        total = total * jnp.concatenate([weight] * 4, axis=1)
        slot = lax.broadcasted_iota(jnp.int32, (CHUNK, FEATURES), 0) + r * CHUNK
        out_ref[r] = jnp.where(slot < count, total, 0.0).astype(BF16)
        result_copy(r).start()

    steps = {"zs": lambda p: z_start(p, 1), "z": z_step, "pj": z_project}
    steps |= {"pk": lambda k, h: z_project(k, h, queries=False), "fin": finish_keys}
    steps |= {"pq": lambda k, h: z_project(k, h, keys=False), "fq": finish_queries}
    steps |= {"kva": kva, "kvb": kvb, "kvc": kvc, "kvd": kvd}
    steps |= {"gq": guest_query, "gw": guest_wait, "gs": guest_send, "gr": guest_return}
    steps |= {"al": attend_many, "ap": attend_pair, "own": own, "at": attend, "ho": heads, "tma": lambda r: terms(r, (3, -3)), "tmb": lambda r: terms(r, (2, -2, 1, -1, 0)), "rs": rs}
    for event in " ".join(SCHEDULE).split():
        name = event.rstrip("0123456789")
        steps[name](*map(int, event[len(name) :]))
    for copy in sends:
        copy.wait_send()
    for r in range(CHUNKS):
        result_copy(r).wait()
    pl.when(lender)(lambda: guest_copy(False).wait_send())
    pl.when(host)(lambda: guest_copy(True).wait_send())


def body(routed_x, norm_gain, w_query, w_key, w_value, w_out, positions, counts, router_weight):
    hbm = pl.BlockSpec(memory_space=pl.ANY)
    smem = pl.BlockSpec(memory_space=pltpu.SMEM)
    return pl.pallas_call(
        kernel,
        out_shape=jax.ShapeDtypeStruct((ROWS, FEATURES), BF16),
        in_specs=[hbm] * 6 + [smem, hbm],
        out_specs=hbm,
        scratch_shapes=[
            pltpu.VMEM((NZ, ROWS, FEATURES), BF16),
            pltpu.VMEM((NZ, 1, FEATURES), F32),
            pltpu.VMEM((CHUNKS, CHUNK), F32),
            pltpu.VMEM((CHUNKS, CHUNK, FEATURES), BF16),
            pltpu.VMEM((NZ * FEATURES, GROUP * HD), BF16),
            pltpu.VMEM((NZ * FEATURES, 2 * HD), BF16),
            pltpu.VMEM((GROUP * HD, NZ * FEATURES), BF16),
            pltpu.VMEM((ROWS, GROUP * HD), F32),
            pltpu.VMEM((ROWS, 2 * HD), F32),
            pltpu.VMEM((ROWS, 128), F32),
            pltpu.VMEM((CHUNKS + 1, Q_ROWS, HD), BF16),
            pltpu.VMEM((CHUNKS, 2, NY, NX, K_TILE, CHUNK), BF16),
            pltpu.VMEM((CHUNKS, 2, NX, NY, CHUNK, HD), BF16),
            pltpu.VMEM((CHUNKS + 1, Q_ROWS, 128), F32),
            pltpu.VMEM((CHUNKS + 1, Q_ROWS, 128), F32),
            pltpu.VMEM((CHUNKS + 1, Q_ROWS, HD), F32),
            pltpu.VMEM((CHUNKS + 1, CHUNK, GROUP * HD), BF16),
            pltpu.VMEM((CHUNKS, 7, CHUNK, FEATURES), F32),
            pltpu.VMEM((2, CHUNKS, 4, CHUNK, FEATURES), BF16),
            pltpu.VMEM((2, CHUNKS, 4, CHUNK, FEATURES), BF16),
            pltpu.SemaphoreType.DMA((7,)),
            pltpu.SemaphoreType.DMA((2, len(PIECES), 4)),
            pltpu.SemaphoreType.DMA((2, len(PIECES), 4)),
            pltpu.SemaphoreType.DMA((CHUNKS, 2, 2, 3)),
            pltpu.SemaphoreType.DMA((CHUNKS, 2, 2, 3)),
            pltpu.SemaphoreType.DMA((CHUNKS, 2, 4)),
            pltpu.SemaphoreType.DMA((CHUNKS, 2, 4)),
            pltpu.SemaphoreType.DMA((2, CHUNKS, 4)),
            pltpu.SemaphoreType.DMA((2, CHUNKS, 4)),
            pltpu.SemaphoreType.DMA((4,)),
            pltpu.SemaphoreType.DMA((CHUNKS,)),
        ],
        compiler_params=pltpu.CompilerParams(
            collective_id=0, has_side_effects=True, vmem_limit_bytes=56 * 1024 * 1024
        ),
    )(
        routed_x,
        norm_gain.reshape(NZ, 1, FEATURES),
        w_query,
        w_key,
        w_value,
        w_out,
        counts,
        router_weight.reshape(CHUNKS, CHUNK),
    )


def solution(mesh):
    return jax.shard_map(
        body,
        mesh=mesh,
        in_specs=(
            P("ctx", "tp"),
            P(),
            P(None, "tp"),
            P(None, "tp"),
            P(None, "tp"),
            P("tp", None),
            P("ctx"),
            P("ctx"),
            P("ctx"),
        ),
        out_specs=P("ctx", "tp"),
        check_vma=False,
    )
```

```python
import jax
import jax.numpy as jnp
from jax import lax
from jax.experimental import pallas as pl
from jax.experimental.pallas import tpu as pltpu
from jax.sharding import PartitionSpec as P

HD = 128
GROUP = 4
ROWS = 384
CHUNK = 128
CHUNKS = 3
FEATURES = 512
Q_ROWS = GROUP * CHUNK
SHARDS = 8
K_TILE = HD + 16
NX, NY, NZ = 4, 4, 8
NEG = -1e30
LOG2E = 1.4426950408889634
BF16 = jnp.bfloat16
F32 = jnp.float32

PIECES = ((0, 64, 0), (64, 64, 0), (128, 64, 1), (192, 64, 1))
PIECES += ((256, 32, 2), (288, 32, 2), (320, 32, 2), (352, 32, 2))
SCHEDULE = (
    "zs0 zs1 zs3 own", "z01 z11 pj01 zs2", "z02 z12 pj02 z31", "z21 pj11 z13 z03",
    "pj03 z32 zs4 zs6", "zs7 z14 zs5 z04", "pj04 fin0 kva0 fq0", "z22 pj12 z33 z41",
    "z71 z61 z23 pj13", "z51 pj21 z34 kvb0", "z72 z62 z42 z24", "pj14 fin1 kva1 fq1",
    "z52 pj22 z73 z63", "z43 z53 pj23 kvb1", "kvc0 z74 z44 z64", "z54 pk24 fin2 kva2",
    "pq24 fq2 gq kvd0", "at00 kvb2 kvc1 gw", "al0 kvd1 at01 kvc2", "al1 kvd2 at02 ho0",
    "rs01 tma0 at32 gs", "at12 rs02 ho1 rs11", "tma1 tmb0 at22 gr", "ho2 rs21 tma2 rs12",
    "rs03 tmb1 rs22 rs13", "rs04 tmb2 rs23 rs14", "rs05 rs24 rs15 rs25",
)


def dot(a, b):
    return jnp.dot(a, b, preferred_element_type=F32)


def kernel(
    x_hbm, gain_hbm, wq_hbm, wk_hbm, wv_hbm, wo_hbm, count_ref, router_hbm, out_hbm,
    xg, gain_ref, router_ref, out_ref, wq, wkv, wo, acc_q, acc_kv, ssq, qs, kt, va, m_s, l_s, o_s, ho, tm, sb, rb,
    w_sem, z_send, z_recv, kv_send, kv_recv, sib_send, sib_recv, rs_send, rs_recv,
    guest_sem, out_sem,
):
    ctx = lax.axis_index("ctx")
    t = lax.axis_index("tp")
    core = lax.rem(ctx, 2)
    y = lax.rem(lax.div(ctx, 2), NY)
    x = lax.div(ctx, 2 * NY)

    def at(xx, yy, cc, tt):
        return ((lax.rem(xx, NX) * NY + lax.rem(yy, NY)) * 2 + cc, lax.rem(tt, NZ))

    z_next = (at(x, y, core, t + 1), at(x, y, core, t + NZ - 1))
    x_line = tuple(at(x + i, y, core, t) for i in (1, 3, 2))
    y_line = tuple(at(x, y + i, core, t) for i in (1, 3, 2))
    sibling = at(x, y, 1 - core, t)
    count = count_ref[0]

    weights = [
        pltpu.make_async_copy(wq_hbm, wq, w_sem.at[0]),
        pltpu.make_async_copy(wk_hbm, wkv.at[:, pl.ds(0, HD)], w_sem.at[1]),
        pltpu.make_async_copy(wv_hbm, wkv.at[:, pl.ds(HD, HD)], w_sem.at[2]),
        pltpu.make_async_copy(gain_hbm, gain_ref, w_sem.at[3]),
        pltpu.make_async_copy(x_hbm, xg.at[t], w_sem.at[4]),
        pltpu.make_async_copy(wo_hbm, wo, w_sem.at[5]),
        pltpu.make_async_copy(router_hbm, router_ref, w_sem.at[6]),
    ]
    for copy in weights:
        copy.start()

    barrier = pltpu.get_barrier_semaphore()
    peers = z_next + x_line + y_line + (sibling,)
    for peer in peers:
        pl.semaphore_signal(barrier, inc=1, device_id=peer, device_id_type=pl.DeviceIdType.MESH)
    pl.semaphore_wait(barrier, len(peers))

    sends = []

    def remote(src, dst, send_sem, recv_sem, device):
        return pltpu.make_async_remote_copy(
            src_ref=src, dst_ref=dst, send_sem=send_sem, recv_sem=recv_sem,
            device_id=device, device_id_type=pl.DeviceIdType.MESH,
        )

    def send(src, dst, send_sem, recv_sem, device):
        copy = remote(src, dst, send_sem, recv_sem, device)
        copy.start()
        sends.append(copy)

    def arrived(dst, send_sem, recv_sem, device):
        remote(dst, dst, send_sem, recv_sem, device).wait_recv()

    def z_rows(d, p, h):
        first, size, chunk = PIECES[p]
        if h < 4:
            return pl.ds(first, size)
        return pl.ds(first + d * (size // 2), size // 2)

    def z_start(p, h):
        for d, sign in enumerate((1, -1)):
            block = lax.rem(t - sign * (h - 1) + NZ, NZ)
            dst = xg.at[block, z_rows(d, p, h)]
            src = x_hbm.at[z_rows(d, p, h)] if h == 1 else dst
            send(src, dst, z_send.at[d, p, h - 1], z_recv.at[d, p, h - 1], z_next[d])

    def project(block, rows, keys, queries):
        widened = xg[block, rows].astype(F32)
        scaled = (widened * gain_ref[block]).astype(BF16)
        features = pl.ds(pl.multiple_of(block * FEATURES, FEATURES), FEATURES)
        if keys:
            squares = widened * widened
            ssq[rows] += sum(squares[:, i * 128 : (i + 1) * 128] for i in range(FEATURES // 128))
            acc_kv[rows] += dot(scaled, wkv[features])
        if queries:
            acc_q[rows] += dot(scaled, wq[features])

    def z_step(p, h):
        for d, sign in enumerate((1, -1)):
            block = lax.rem(t - sign * h + NZ, NZ)
            arrived(
                xg.at[block, z_rows(d, p, h)], z_send.at[d, p, h - 1], z_recv.at[d, p, h - 1], z_next[d]
            )
        if h < 4:
            z_start(p, h + 1)

    def z_project(k, h, keys=True, queries=True):
        for sign in (1, -1) if h < 4 else (1,):
            block = lax.rem(t - sign * h + NZ, NZ)
            project(block, pl.ds(k * CHUNK, CHUNK), keys, queries)

    def own():
        for copy in weights[:5]:
            copy.wait()
        ssq[...] = jnp.zeros_like(ssq)
        acc_q[...] = jnp.zeros_like(acc_q)
        acc_kv[...] = jnp.zeros_like(acc_kv)
        m_s[...] = jnp.full_like(m_s, NEG)
        l_s[...] = jnp.zeros_like(l_s)
        o_s[...] = jnp.zeros_like(o_s)
        project(t, pl.ds(0, ROWS), True, True)

    def row_scale(rows):
        mean = jnp.sum(ssq[rows], axis=1, keepdims=True) * (1.0 / (NZ * FEATURES))
        return lax.rsqrt(mean + 1e-05)

    def finish_queries(k):
        rows = pl.ds(k * CHUNK, CHUNK)
        query = (acc_q[rows] * (row_scale(rows) * (HD**-0.5 * LOG2E))).astype(BF16)
        for h in range(GROUP):
            qs[k, h * CHUNK : (h + 1) * CHUNK, :] = query[:, h * HD : (h + 1) * HD]

    def finish_keys(k):
        rows = pl.ds(k * CHUNK, CHUNK)
        pair = acc_kv[rows] * row_scale(rows)
        kt[k, core, y, x, 0:HD, :] = jnp.transpose(pair[:, :HD]).astype(BF16)
        slot = lax.broadcasted_iota(jnp.int32, (16, CHUNK), 1) + k * CHUNK
        kt[k, core, y, x, HD:K_TILE, :] = jnp.where(slot < count, 0.0, NEG).astype(BF16)
        va[k, core, x, y, :, :] = pair[:, HD:].astype(BF16)

    kinds = ((kt, x, y, x_line, y_line), (va, y, x, y_line, x_line))

    def kv_sems(k, a, phase, i):
        return kv_send.at[k, a, phase, i], kv_recv.at[k, a, phase, i]

    def kva(k):
        for a, (buf, inner, outer, inner_line, outer_line) in enumerate(kinds):
            tile = buf.at[k, core, outer, inner]
            for i in range(3):
                send(tile, tile, *kv_sems(k, a, 0, i), inner_line[i])

    def kvb(k):
        for a, (buf, inner, outer, inner_line, outer_line) in enumerate(kinds):
            for i in range(3):
                tile = buf.at[k, core, outer, lax.rem(inner + (3, 1, 2)[i], 4)]
                arrived(tile, *kv_sems(k, a, 0, i), inner_line[i])
            line = buf.at[k, core, outer]
            for i in range(3):
                send(line, line, *kv_sems(k, a, 1, i), outer_line[i])
            send(line, line, sib_send.at[k, a, 3], sib_recv.at[k, a, 3], sibling)

    def kvc(k):
        for i in range(3):
            for a, (buf, inner, outer, inner_line, outer_line) in enumerate(kinds):
                line = buf.at[k, core, lax.rem(outer + (3, 1, 2)[i], 4)]
                arrived(line, *kv_sems(k, a, 1, i), outer_line[i])
                send(line, line, sib_send.at[k, a, i], sib_recv.at[k, a, i], sibling)

    def kvd(k):
        for a, (buf, inner, outer, inner_line, outer_line) in enumerate(kinds):
            for i in range(4):
                line = buf.at[k, 1 - core, lax.rem(outer + (3, 1, 2, 0)[i], 4)]
                arrived(line, sib_send.at[k, a, i], sib_recv.at[k, a, i], sibling)

    place = lax.rem(ctx, SHARDS)
    host, lender = x == 0, x == NX - 1

    def absorb(r, chunk, j, g, last, pair=False):
        count_rows = 2 * Q_ROWS if pair else Q_ROWS
        slot = lax.rem(lax.broadcasted_iota(jnp.int32, (count_rows, CHUNK), 0), CHUNK)
        if pair:
            half_rows = lax.broadcasted_iota(jnp.int32, (count_rows, CHUNK), 0)
            slot = jnp.where(half_rows < Q_ROWS, slot, slot + CHUNK)
        slot = slot.astype(F32)

        def rows_of(ref):
            return ref[0:2].reshape(count_rows, HD) if pair else ref[r]

        def put(ref, value):
            if pair:
                ref[0:2] = value.reshape(2, Q_ROWS, HD)
            else:
                ref[r] = value

        column = lax.broadcasted_iota(jnp.int32, (1, CHUNK), 1)
        keys, first, values = [], [], []
        own_limit = jnp.where(j < chunk, CHUNK, jnp.where(j == chunk, 0, -CHUNK))
        if pair:
            own_limit = -j * CHUNK
        for i in range(SHARDS):
            keys.append(kt[j, i % 2, i // 2, g, 0:HD, :])
            mask = kt[j, i % 2, i // 2, g, HD:K_TILE, :].astype(F32)[0:1, :]
            limit = jnp.where(i < place, ROWS, jnp.where(i == place, own_limit, -ROWS))
            limit = jnp.where(g < last, ROWS, limit)
            first.append(jnp.where(mask < 0.0, 1e9, (column - limit).astype(F32)))
            values.append(va[j, i % 2, g, i // 2, :, :])
        scores = dot(rows_of(qs), jnp.concatenate(keys, axis=1))
        scores = [
            jnp.where(first[i] <= slot, scores[:, i * CHUNK : (i + 1) * CHUNK], NEG)
            for i in range(SHARDS)
        ]
        scores = jnp.concatenate(scores, axis=1)
        before = rows_of(m_s)
        after = jnp.maximum(before, jnp.max(scores, axis=1, keepdims=True))
        factor = jnp.exp2(before - after)
        probs = jnp.exp2(scores - jnp.concatenate([after] * SHARDS, axis=1))
        put(m_s, after)
        lanes = sum(probs[:, i * CHUNK : (i + 1) * CHUNK] for i in range(SHARDS))
        put(l_s, rows_of(l_s) * factor + lanes)
        mixed = dot(probs.astype(BF16), jnp.concatenate(values, axis=0))
        put(o_s, rows_of(o_s) * factor + mixed)

    def attend(r, j):
        guest = jnp.int32(r) == 3
        lent = (jnp.int32(r) == 2) & lender
        last = jnp.where(guest, NX - 1, x)
        groups = jnp.where(guest, jnp.where(host, NX, 0), jnp.where(lent, 0, x + 1))
        chunk = jnp.minimum(jnp.int32(r), 2)

        pairs = lax.div(groups, 2)

        @pl.loop(0, pairs)
        def _(i):
            absorb(r, chunk, jnp.int32(j), 2 * i, last)
            absorb(r, chunk, jnp.int32(j), 2 * i + 1, last)

        @pl.loop(2 * pairs, groups)
        def _(g):
            absorb(r, chunk, jnp.int32(j), g, last)

    def attend_many(j):
        pl.loop(1, 4)(lambda r: attend(r, j))

    def guest_copy(back):
        i = 1 if back else 0
        src = ho.at[3] if back else qs.at[2]
        dst = ho.at[2] if back else qs.at[3]
        return remote(src, dst, guest_sem.at[i], guest_sem.at[2 + i], x_line[i])

    def guest_query():
        pl.when(lender)(lambda: guest_copy(False).start())

    def guest_wait():
        pl.when(host)(lambda: guest_copy(False).wait_recv())

    def guest_send():
        @pl.when(host)
        def _():
            mix(3)
            guest_copy(True).start()

    def guest_return():
        pl.when(lender)(lambda: guest_copy(True).wait_recv())

    def mix(r):
        mixed = (o_s[r] / jnp.sum(l_s[r], axis=1, keepdims=True)).astype(BF16)
        for h in range(GROUP):
            ho[r, :, h * HD : (h + 1) * HD] = mixed[h * CHUNK : (h + 1) * CHUNK, :]

    def heads(r):
        if r == 0:
            weights[5].wait()
            weights[6].wait()
        if r == 2:
            pl.when(jnp.logical_not(lender))(lambda: mix(2))
        else:
            mix(r)

    def term(r, block):
        block = lax.rem(block + NZ, NZ)
        columns = pl.ds(pl.multiple_of(block * FEATURES, FEATURES), FEATURES)
        return dot(ho[r], wo[:, columns])

    half = CHUNK // 2

    def result_copy(r):
        return pltpu.make_async_copy(
            out_ref.at[r], out_hbm.at[pl.ds(r * CHUNK, CHUNK)], out_sem.at[r]
        )

    def terms(r, shifts):
        for shift in shifts:
            tm[r, shift + 3] = term(r, t + shift)

    def rs(r, step):
        def rs_sems(d, hop):
            return rs_send.at[d, r, hop], rs_recv.at[d, r, hop]

        def rows(d, hop):
            return pl.ds(d * half, half) if hop == 0 else pl.ds(0, CHUNK)

        if step == 1:
            product = term(r, t + 4).astype(BF16)
            for d in range(2):
                sb[d, r, 0, rows(d, 0)] = product[d * half : (d + 1) * half]
        for d, sign in enumerate((1, -1)):
            if step == 5:
                break
            if step > 1:
                product = tm.at[r, 3 + sign * (5 - step)]
                landed = rb.at[d, r, step - 2, rows(d, step - 2)]
                arrived(landed, *rs_sems(d, step - 2), z_next[d])
                if step == 2:
                    sb[d, r, 1, rows(1 - d, 0)] = product[rows(1 - d, 0)].astype(BF16)
                add = product[rows(d, step - 2)] + landed[...].astype(F32)
                sb[d, r, step - 1, rows(d, step - 2)] = add.astype(BF16)
            src = sb.at[d, r, step - 1, rows(d, step - 1)]
            dst = rb.at[d, r, step - 1, rows(d, step - 1)]
            send(src, dst, *rs_sems(d, step - 1), z_next[d])
        if step < 5:
            return
        total = tm[r, 3]
        for d in range(2):
            landed = rb.at[d, r, 3]
            arrived(landed, *rs_sems(d, 3), z_next[d])
            total = total + landed[...].astype(F32)
        weight = jnp.transpose(jnp.broadcast_to(router_ref[r : r + 1, :], (CHUNK, CHUNK)))
        total = total * jnp.concatenate([weight] * 4, axis=1)
        slot = lax.broadcasted_iota(jnp.int32, (CHUNK, FEATURES), 0) + r * CHUNK
        out_ref[r] = jnp.where(slot < count, total, 0.0).astype(BF16)
        result_copy(r).start()

    steps = {"zs": lambda p: z_start(p, 1), "z": z_step, "pj": z_project}
    steps |= {"pk": lambda k, h: z_project(k, h, queries=False), "fin": finish_keys}
    steps |= {"pq": lambda k, h: z_project(k, h, keys=False), "fq": finish_queries}
    steps |= {"kva": kva, "kvb": kvb, "kvc": kvc, "kvd": kvd}
    steps |= {"gq": guest_query, "gw": guest_wait, "gs": guest_send, "gr": guest_return}
    steps |= {"al": attend_many, "own": own, "at": attend, "ho": heads, "tma": lambda r: terms(r, (3, -3)), "tmb": lambda r: terms(r, (2, -2, 1, -1, 0)), "rs": rs}
    for event in " ".join(SCHEDULE).split():
        name = event.rstrip("0123456789")
        steps[name](*map(int, event[len(name) :]))
    for copy in sends:
        copy.wait_send()
    for r in range(CHUNKS):
        result_copy(r).wait()
    pl.when(lender)(lambda: guest_copy(False).wait_send())
    pl.when(host)(lambda: guest_copy(True).wait_send())


def body(routed_x, norm_gain, w_query, w_key, w_value, w_out, positions, counts, router_weight):
    hbm = pl.BlockSpec(memory_space=pl.ANY)
    smem = pl.BlockSpec(memory_space=pltpu.SMEM)
    return pl.pallas_call(
        kernel,
        out_shape=jax.ShapeDtypeStruct((ROWS, FEATURES), BF16),
        in_specs=[hbm] * 6 + [smem, hbm],
        out_specs=hbm,
        scratch_shapes=[
            pltpu.VMEM((NZ, ROWS, FEATURES), BF16),
            pltpu.VMEM((NZ, 1, FEATURES), F32),
            pltpu.VMEM((CHUNKS, CHUNK), F32),
            pltpu.VMEM((CHUNKS, CHUNK, FEATURES), BF16),
            pltpu.VMEM((NZ * FEATURES, GROUP * HD), BF16),
            pltpu.VMEM((NZ * FEATURES, 2 * HD), BF16),
            pltpu.VMEM((GROUP * HD, NZ * FEATURES), BF16),
            pltpu.VMEM((ROWS, GROUP * HD), F32),
            pltpu.VMEM((ROWS, 2 * HD), F32),
            pltpu.VMEM((ROWS, 128), F32),
            pltpu.VMEM((CHUNKS + 1, Q_ROWS, HD), BF16),
            pltpu.VMEM((CHUNKS, 2, NY, NX, K_TILE, CHUNK), BF16),
            pltpu.VMEM((CHUNKS, 2, NX, NY, CHUNK, HD), BF16),
            pltpu.VMEM((CHUNKS + 1, Q_ROWS, 128), F32),
            pltpu.VMEM((CHUNKS + 1, Q_ROWS, 128), F32),
            pltpu.VMEM((CHUNKS + 1, Q_ROWS, HD), F32),
            pltpu.VMEM((CHUNKS + 1, CHUNK, GROUP * HD), BF16),
            pltpu.VMEM((CHUNKS, 7, CHUNK, FEATURES), F32),
            pltpu.VMEM((2, CHUNKS, 4, CHUNK, FEATURES), BF16),
            pltpu.VMEM((2, CHUNKS, 4, CHUNK, FEATURES), BF16),
            pltpu.SemaphoreType.DMA((7,)),
            pltpu.SemaphoreType.DMA((2, len(PIECES), 4)),
            pltpu.SemaphoreType.DMA((2, len(PIECES), 4)),
            pltpu.SemaphoreType.DMA((CHUNKS, 2, 2, 3)),
            pltpu.SemaphoreType.DMA((CHUNKS, 2, 2, 3)),
            pltpu.SemaphoreType.DMA((CHUNKS, 2, 4)),
            pltpu.SemaphoreType.DMA((CHUNKS, 2, 4)),
            pltpu.SemaphoreType.DMA((2, CHUNKS, 4)),
            pltpu.SemaphoreType.DMA((2, CHUNKS, 4)),
            pltpu.SemaphoreType.DMA((4,)),
            pltpu.SemaphoreType.DMA((CHUNKS,)),
        ],
        compiler_params=pltpu.CompilerParams(
            collective_id=0, has_side_effects=True, vmem_limit_bytes=56 * 1024 * 1024
        ),
    )(
        routed_x,
        norm_gain.reshape(NZ, 1, FEATURES),
        w_query,
        w_key,
        w_value,
        w_out,
        counts,
        router_weight.reshape(CHUNKS, CHUNK),
    )


def solution(mesh):
    return jax.shard_map(
        body,
        mesh=mesh,
        in_specs=(
            P("ctx", "tp"),
            P(),
            P(None, "tp"),
            P(None, "tp"),
            P(None, "tp"),
            P("tp", None),
            P("ctx"),
            P("ctx"),
            P("ctx"),
        ),
        out_specs=P("ctx", "tp"),
        check_vma=False,
    )
```
